256 devices in a mesh: row: 32 (over z, y_hi, core), col: 8 (over x, y_lo).
Axes of the slice: x: 4, y: 4 (y_hi: 2, y_lo: 2; y = y_hi * 2 + y_lo), z: 8, core: 2. Of those that a mesh axis runs over, the one named last changes fastest.
Arguments:
- start_prev: float32 [512, 1024, 128], P('row', 'col'), may hold values from -6 to 6
- start_cur: float32 [512, 1024, 128], P('row', 'col'), may hold values from -6 to 6
- adj_prev: float32 [512, 1024, 128], P('row', 'col'), may hold values from -6 to 6
- adj_cur: float32 [512, 1024, 128], P('row', 'col'), may hold values from -6 to 6
- material: int32 [512, 1024, 128], P('row', 'col'), may hold values from 0 to 7
- speed_sq: float32 [8], replicated, may hold values from 0.08 to 0.32
- admittance: float32 [8, 2048], P('col', 'row'), may hold values from 0.2 to 2
- bound_cell: int32 [32, 16384], P('row', 'col'), may hold values from -1 to 262143, as said below
- bound_patch: int32 [32, 16384], P('row', 'col'), may hold values from -1 to 2047, as said below
Outputs:
- grad_prev: float32 [512, 1024, 128], P('row', 'col')
- grad_cur: float32 [512, 1024, 128], P('row', 'col')
- patch_grad: float32 [8, 2048], P('col', 'row')
The draws below stay inside these ranges and needn't reach their ends.
Inputs may be any that keep to these rules, and one draw needn't show every extreme that they name: `bound_cell`: in each block's 2048 entries the live ones come first, in rising order and distinct, as flat indices x * 128 * 128 + y * 128 + z of cells inside that block; the rest are -1. Every block has at least 1024 live entries, and some block has all 2048. `bound_patch`: -1 exactly where bound_cell is -1.
All inputs are finite; a program needn't handle non-finite values.
Results may differ from the reference program's by a relative error of at most 0.00002.
Values sent between devices are 32-bit elements; how exact they have to be, the bound alone decides.
A program may use at most 64 MiB of HBM per device.

```python
import math
import jax
import jax.numpy as jnp

CX = 16
CY = 128
NZ = 128
SLOTS = 2048
STEPS = 4
MATS = 8
BLOCKS_X = 32
STRIPS = 8
NX = 512
NY = 1024
PATCH_STRIP = 2048


def boundary_lists(key):
    base = jax.random.fold_in(key, 11)
    key_count, key_offset, key_patch, key_full = jax.random.split(base, 4)
    cells_dev = CX * CY * NZ
    stride = cells_dev // SLOTS
    blocks = BLOCKS_X * STRIPS
    counts = jax.random.randint(key_count, (blocks,), SLOTS // 2, SLOTS)
    full_block = jax.random.randint(key_full, (), 0, blocks)
    block_ids = jnp.arange(blocks)
    is_full = block_ids == full_block
    counts = jnp.where(is_full, SLOTS, counts)
    slot_ids = jnp.arange(SLOTS)[None, :]
    offsets = jax.random.randint(key_offset, (blocks, SLOTS), 0, stride)
    offsets = jnp.where(is_full[:, None] & (slot_ids == SLOTS - 1), stride - 1, offsets)
    live = slot_ids < counts[:, None]
    cells = jnp.where(live, slot_ids * stride + offsets, -1)
    patches = jax.random.randint(key_patch, (blocks, SLOTS), 0, PATCH_STRIP)
    patches = jnp.where(is_full[:, None] & (slot_ids == 0), PATCH_STRIP - 1, patches)
    patches = jnp.where(live, patches, -1)
    cells = cells.reshape(BLOCKS_X, STRIPS * SLOTS).astype(jnp.int32)
    patches = patches.reshape(BLOCKS_X, STRIPS * SLOTS).astype(jnp.int32)
    return (cells, patches)


def draw_bound_cell(key, part):
    return boundary_lists(key)[0]


def draw_bound_patch(key, part):
    return boundary_lists(key)[1]


def plant(result, key, least, high):
    index_at = [jax.random.randint(jax.random.fold_in(key, axis), (), 0, length) for axis, length in enumerate(result.shape)]
    longest = result.shape.index(max(result.shape))
    beside = index_at[:longest] + [(index_at[longest] + 1) % result.shape[longest]] + index_at[longest + 1:]
    return result.at[tuple(index_at)].set(least).at[tuple(beside)].set(high)


def level_of(rng, shape, cuts, least, largest):
    loudness, own = 1.0, jax.random.fold_in(rng, 6)
    for position, blocks in cuts:
        heights = jnp.exp(jax.random.uniform(jax.random.fold_in(own, position), (blocks,), jnp.float32, least / len(cuts), largest / len(cuts)))
        loudness = loudness * jnp.repeat(heights, shape[position] // blocks).reshape([-1 if axis == position else 1 for axis in range(len(shape))])
    return loudness


def normal_values(stream_key, shape, scale, bound, cuts=(), kind=jnp.bfloat16):
    level = level_of(stream_key, shape, cuts, -0.22, 0.18) if cuts else 1.0
    drawn = jax.random.normal(stream_key, shape, jnp.float32) * scale * level
    return jnp.minimum(jnp.maximum(drawn, -bound), bound).astype(kind)


def setup_inputs(seed: int = 0) -> dict:
    seeds = jax.random.split(jax.random.key(seed), 10)
    return {
        "start_prev": normal_values(seeds[0], (NX, NY, NZ), 1.0, 6.0, ((0, 32), (1, 8)), jnp.float32),
        "start_cur": normal_values(seeds[1], (NX, NY, NZ), 1.0, 6.0, ((0, 32), (1, 8)), jnp.float32),
        "adj_prev": normal_values(seeds[2], (NX, NY, NZ), 1.0, 6.0, ((0, 32), (1, 8)), jnp.float32),
        "adj_cur": normal_values(seeds[3], (NX, NY, NZ), 1.0, 6.0, ((0, 32), (1, 8)), jnp.float32),
        "material": plant(jax.random.randint(seeds[4], (NX, NY, NZ), 0, MATS), jax.random.fold_in(seeds[4], 1), 0, MATS - 1).astype(jnp.int32),
        "speed_sq": jnp.clip(jnp.exp(jax.random.uniform(seeds[5], (MATS,), jnp.float32, math.log(0.08), math.log(0.32))), 0.08, 0.32),
        "admittance": jnp.clip(jnp.exp(math.log(2.0) - 2.3025851 * jax.random.uniform(seeds[6], (STRIPS, PATCH_STRIP), jnp.float32) ** level_of(seeds[6], (STRIPS, PATCH_STRIP), ((0, 8), (1, 32)), -0.2, 0.2)), 0.2, 2.0),
        "bound_cell": draw_bound_cell(jax.random.fold_in(seeds[9], 71), 0),
        "bound_patch": draw_bound_patch(jax.random.fold_in(seeds[9], 71), 0),
    }


def neighbour_sum(field):
    padded = jnp.pad(field, 1)
    total = padded[2:, 1:-1, 1:-1] + padded[:-2, 1:-1, 1:-1]
    total = total + padded[1:-1, 2:, 1:-1] + padded[1:-1, :-2, 1:-1]
    total = total + padded[1:-1, 1:-1, 2:] + padded[1:-1, 1:-1, :-2]
    return total


def laplace(field):
    return neighbour_sum(field) - 6.0 * field


def reference(start_prev, start_cur, adj_prev, adj_cur, material, speed_sq, admittance, bound_cell, bound_patch):
    c2 = speed_sq[material]
    cells = bound_cell.reshape(BLOCKS_X, STRIPS, SLOTS)
    patches = bound_patch.reshape(BLOCKS_X, STRIPS, SLOTS)
    live = cells >= 0
    safe_cell = jnp.maximum(cells, 0).astype(jnp.int32)
    safe_patch = jnp.maximum(patches, 0).astype(jnp.int32)
    block_x = jnp.arange(BLOCKS_X).astype(jnp.int32)[:, None, None]
    strip_y = jnp.broadcast_to(jnp.arange(STRIPS).astype(jnp.int32)[None, :, None], safe_cell.shape)
    pos_x = block_x * CX + safe_cell // (CY * NZ)
    pos_y = strip_y * CY + (safe_cell // NZ) % CY
    pos_z = safe_cell % NZ
    flat = ((pos_x * NY + pos_y) * NZ + pos_z).astype(jnp.int32)
    slot_gamma = jnp.where(live, 0.25 * admittance[strip_y, safe_patch], jnp.float32(0.0))
    gamma = jnp.zeros((NX * NY * NZ,), jnp.float32).at[flat.reshape(-1)].add(slot_gamma.reshape(-1))
    gamma = gamma.reshape(NX, NY, NZ)
    states = [start_prev, start_cur]
    for step in range(STEPS):
        prev = states[-2]
        cur = states[-1]
        drive = 2.0 * cur + c2 * laplace(cur)
        states.append((drive - (1.0 - gamma) * prev) / (1.0 + gamma))
    m_low = adj_prev
    m_high = adj_cur
    grad_gamma = jnp.zeros_like(start_prev)
    for level in range(STEPS, 0, -1):
        weight = m_high / (1.0 + gamma)
        grad_gamma = grad_gamma + weight * (states[level - 1] - states[level + 1])
        m_new = m_low + 2.0 * weight + laplace(c2 * weight)
        m_low = -(1.0 - gamma) * weight
        m_high = m_new
    values = jnp.where(live, 0.25 * grad_gamma.reshape(-1)[flat], jnp.float32(0.0))
    patch_grad = jnp.zeros((STRIPS, PATCH_STRIP), jnp.float32).at[strip_y, safe_patch].add(values)
    return m_low, m_high, patch_grad
```

```python
import jax
import jax.numpy as jnp
from jax import lax
from jax.experimental import pallas as pl
from jax.experimental.pallas import tpu as pltpu
from jax.sharding import PartitionSpec as P

MESH = pl.DeviceIdType.MESH
F32 = jnp.float32
BF16 = jnp.bfloat16
CX, CY, NZ = 16, 128, 128
SLOTS = 2048
ROWS = 32
COLS = 8
SHARE = 64
PX, PY = CX + 2, CY + 16


def natural(step):
    return pl.ds(step, 8, 16)


def lane_masks():
    lane = lax.broadcasted_iota(jnp.int32, (8, NZ), 1)
    return lane == 0, lane == NZ - 1


def around(field, x, row, masks):
    here = field[x, pl.ds(row, 8), :]
    total = field[x - 1, pl.ds(row, 8), :] + field[x + 1, pl.ds(row, 8), :]
    total = total + (field[x, pl.ds(row - 8, 8), :] + field[x, pl.ds(row + 8, 8), :])
    low = jnp.where(masks[0], 0.0, pltpu.roll(here, 1, 1))
    high = jnp.where(masks[1], 0.0, pltpu.roll(here, NZ - 1, 1))
    return here, total + (low + high) - 6.0 * here


def fill_sides(field, x):
    field[x, 1:8, :] = field[x, CY : CY + 7, :]
    field[x, CY + 8 : CY + 15, :] = field[x, 9:16, :]


def kernel(
    p0_in, p1_in, m4_in, m5_in, mat_in, speed, adm, cell, patch,
    g0_out, g1_out, pg_out,
    raw, kinds, fields, c2, q, before, base, diff, weights, last, result,
    side, rt, bt, vt, gt, gsum, own, table, parts, arrived,
    load_sem, store_sem, send_sem, recv_sem, share_sem,
):
    row = lax.axis_index("row")
    col = lax.axis_index("col")
    masks = lane_masks()

    names = (p1_in, mat_in, p0_in, m5_in, m4_in)
    loads = [
        pltpu.make_async_copy(ref, kinds if n == 1 else raw.at[n], load_sem.at[n])
        for n, ref in enumerate(names)
    ]
    for load in loads:
        load.start()

    barrier = pltpu.get_barrier_semaphore()

    def greet(step, carry):
        pl.semaphore_signal(
            barrier, inc=1, device_id=(lax.rem(row + step, ROWS), col), device_id_type=MESH
        )
        return carry

    lax.fori_loop(1, ROWS, greet, 0)
    for step in (1, COLS - 1):
        pl.semaphore_signal(
            barrier, inc=1, device_id=(row, lax.rem(col + step, COLS)), device_id_type=MESH
        )

    zero_plane = jnp.zeros((CY, NZ), F32)
    zero_row = jnp.zeros((CX, 1, NZ), F32)

    @pl.when(row == 0)
    def _():
        for f in range(8):
            fields[f, 0, 8 : 8 + CY, :] = zero_plane

    @pl.when(row == ROWS - 1)
    def _():
        for f in range(8):
            fields[f, PX - 1, 8 : 8 + CY, :] = zero_plane

    @pl.when(col == 0)
    def _():
        for f in range(8):
            fields[f, 1 : 1 + CX, 0:1, :] = zero_row

    @pl.when(col == COLS - 1)
    def _():
        for f in range(8):
            fields[f, 1 : 1 + CX, PY - 1 : PY, :] = zero_row

    own[...] = jnp.zeros_like(own)
    own[0, :, 0:SHARE] = adm[...]
    table[pl.ds(row, 1)] = own[...]

    pl.semaphore_wait(barrier, ROWS + 1)

    sides = (
        (row < ROWS - 1, (row + 1, col)),
        (row > 0, (row - 1, col)),
        (col < COLS - 1, (row, col + 1)),
        (col > 0, (row, col - 1)),
    )
    comes = (row > 0, row < ROWS - 1, col > 0, col < COLS - 1)

    def copies(f):
        field = fields.at[f]
        pairs = (
            (field.at[CX, 8 : 8 + CY, :], field.at[0, 8 : 8 + CY, :]),
            (field.at[1, 8 : 8 + CY, :], field.at[PX - 1, 8 : 8 + CY, :]),
            (field.at[1 : 1 + CX, CY + 7 : CY + 8, :], field.at[1 : 1 + CX, 0:1, :]),
            (field.at[1 : 1 + CX, 8:9, :], field.at[1 : 1 + CX, PY - 1 : PY, :]),
        )
        if f == 0:
            pairs = (
                (p1_in.at[CX - 1], side.at[0]),
                (p1_in.at[0], side.at[1]),
                (p1_in.at[:, CY - 1 : CY, :], pairs[2][1]),
                (p1_in.at[:, 0:1, :], pairs[3][1]),
            )
        return [
            pltpu.make_async_remote_copy(
                src, dst, send_sem.at[f, d], recv_sem.at[f, d],
                device_id=sides[d][1], device_id_type=MESH,
            )
            for d, (src, dst) in enumerate(pairs)
        ]

    def send(f):
        for d, copy in enumerate(copies(f)):
            pl.when(sides[d][0])(copy.start)

    def receive(f):
        for d, copy in enumerate(copies(f)):
            pl.when(comes[d])(copy.wait_recv)

    def sent(f):
        for d, copy in enumerate(copies(f)):
            pl.when(sides[d][0])(copy.wait_send)

    send(0)

    def share(source, sem):
        def start(step, carry):
            to = lax.rem(row + step, ROWS)
            pltpu.make_async_remote_copy(
                source(to), (table if sem == 0 else arrived).at[pl.ds(row, 1)],
                share_sem.at[2 * sem], share_sem.at[2 * sem + 1],
                device_id=(to, col), device_id_type=MESH,
            ).start()
            return carry

        lax.fori_loop(1, ROWS, start, 0)

    def shared(buffer, which):
        rest = buffer.at[pl.ds(0, ROWS - 1)]
        pltpu.make_async_copy(rest, rest, share_sem.at[which]).wait()

    share(lambda to: own, 0)

    cells = cell[...]
    spots = patch[...]
    depth = cells & (NZ - 1)
    y = (cells >> 7) & (CY - 1)
    line = (cells >> 14) * CY + (y & 15) * 8 + (y >> 4)
    owner = spots >> 6
    place = spots & (SHARE - 1)

    def build(block, carry):
        start = pl.multiple_of(block * 16, 16)
        index = lax.broadcasted_iota(jnp.int32, (16, SLOTS), 0) + start
        rt[pl.ds(start, 16), :] = jnp.where(index == line, 1.0, 0.0).astype(BF16)
        return carry

    lax.fori_loop(0, SLOTS // 16, build, 0)
    index = lax.broadcasted_iota(jnp.int32, (NZ, SLOTS), 0)
    bt[...] = jnp.where(index == place, 1.0, 0.0).astype(BF16)

    loads[0].wait()
    loads[1].wait()
    speeds = [speed[n] for n in range(8)]

    def arrange(x, carry):
        for t in range(16):
            fields[0, x + 1, pl.ds(8 + 8 * t, 8), :] = raw[0, x, natural(t), :]
            kind = kinds[x, natural(t), :]
            value = jnp.full((8, NZ), speeds[0], F32)
            for n in range(1, 8):
                value = jnp.where(kind == n, speeds[n], value)
            c2[x, pl.ds(8 * t, 8), :] = value
        fill_sides(fields.at[0], x + 1)
        return carry

    lax.fori_loop(0, CX, arrange, 0)

    loads[2].wait()
    loads[3].wait()
    loads[4].wait()

    def arrange_rest(x, carry):
        for t in range(16):
            before[x, pl.ds(8 * t, 8), :] = raw[2, x, natural(t), :]
        return carry

    lax.fori_loop(0, CX, arrange_rest, 0)

    shared(table, 1)
    shared(table, 0)
    strip = 0.25 * table[:, 0, :]
    strip_high = strip.astype(BF16)
    strip_low = (strip - strip_high.astype(F32)).astype(BF16)
    found = jnp.dot(
        jnp.concatenate([strip_high, strip_low], axis=0), bt[...], preferred_element_type=F32
    )
    found = found[:ROWS] + found[ROWS:]
    index = lax.broadcasted_iota(jnp.int32, (ROWS, SLOTS), 0)
    slot = jnp.sum(jnp.where(index == owner, found, 0.0), axis=0, keepdims=True)
    slot_high = slot.astype(BF16).astype(F32)
    slot_low = slot - slot_high
    index = lax.broadcasted_iota(jnp.int32, (NZ, SLOTS), 0)
    vt[0:NZ, :] = jnp.where(index == depth, slot_high, 0.0).astype(BF16)
    vt[NZ : 2 * NZ, :] = jnp.where(index == depth, slot_low, 0.0).astype(BF16)

    def spread(pair, carry):
        start = pl.multiple_of(pair * 256, 256)
        both = lax.dot_general(
            rt[pl.ds(start, 256), :], vt[...], (((1,), (1,)), ((), ())), preferred_element_type=F32
        )
        for half in range(2):
            x = 2 * pair + half
            for t in range(16):
                at = half * CY + 8 * t
                gamma = both[at : at + 8, 0:NZ] + both[at : at + 8, NZ : 2 * NZ]
                here = pl.ds(8 * t, 8)
                scale = 1.0 / (1.0 + gamma)
                q[x, here, :] = scale
                high = raw[3, x, natural(t), :]
                weight = scale * high
                weights[0, x, here, :] = weight
                fields[4, x + 1, pl.ds(8 + 8 * t, 8), :] = c2[x, here, :] * weight
                base[x, here, :] = raw[4, x, natural(t), :] + 2.0 * weight
                diff[x, here, :] = high - 2.0 * weight
            fill_sides(fields.at[4], x + 1)
        return carry

    lax.fori_loop(0, CX // 2, spread, 0)
    send(4)

    def forward(k):
        now = fields.at[k - 1]

        def tile(x, t):
            at = pl.ds(8 * t, 8)
            here, change = around(now, x, 8 + 8 * t, masks)
            old = before[x - 1, at, :] if k == 1 else fields[k - 2, x, pl.ds(8 + 8 * t, 8), :]
            new = old + q[x - 1, at, :] * (2.0 * (here - old) + c2[x - 1, at, :] * change)
            if k == 4:
                last[x - 1, at, :] = new
            else:
                fields[k, x, pl.ds(8 + 8 * t, 8), :] = new

        def done(x):
            if k < 4:
                fill_sides(fields.at[k], x)

        return tile, done

    def adjoint(k):
        f = 8 - k
        now = fields.at[f]

        def tile(x, t):
            at = pl.ds(8 * t, 8)
            here, change = around(now, x, 8 + 8 * t, masks)
            high = base[x - 1, at, :] + change
            if k == 1:
                result[1, x - 1, natural(t), :] = high
                return
            weight = q[x - 1, at, :] * high
            weights[f - 3, x - 1, at, :] = weight
            fields[f + 1, x, pl.ds(8 + 8 * t, 8), :] = c2[x - 1, at, :] * weight
            twice = 2.0 * weight
            base[x - 1, at, :] = diff[x - 1, at, :] + twice
            if k == 2:
                result[0, x - 1, natural(t), :] = high - twice
            else:
                diff[x - 1, at, :] = high - twice

        def done(x):
            if k > 1:
                fill_sides(fields.at[f + 1], x)

        return tile, done

    def inside(step):
        def body(x, carry):
            for t in range(1, 15):
                step[0](x, t)
            return carry

        lax.fori_loop(2, CX, body, 0)

    def outside(step):
        def ends(n, carry):
            x = 1 + n * (CX - 1)
            for t in range(16):
                step[0](x, t)
            step[1](x)
            return carry

        def edges(x, carry):
            for t in (0, 15):
                step[0](x, t)
            step[1](x)
            return carry

        lax.fori_loop(0, 2, ends, 0)
        lax.fori_loop(2, CX, edges, 0)

    inside(forward(1))
    receive(0)
    for n, plane, there in ((0, 0, comes[0]), (1, PX - 1, comes[1])):
        def place_side(n=n, plane=plane):
            for t in range(16):
                fields[0, plane, pl.ds(8 + 8 * t, 8), :] = side[n, natural(t), :]

        pl.when(there)(place_side)
    outside(forward(1))
    send(1)

    for k in (2, 3, 4):
        level = 6 - k
        step = adjoint(level)
        inside(step)
        receive(8 - level)
        outside(step)
        send(9 - level)
        step = forward(k)
        inside(step)
        receive(k - 1)
        outside(step)
        if k < 4:
            send(k)

    first_store = pltpu.make_async_copy(result.at[0], g0_out, store_sem.at[0])
    first_store.start()

    def collect(x, carry):
        for t in range(16):
            at = pl.ds(8 * t, 8)
            inner = pl.ds(8 + 8 * t, 8)
            total = weights[3, x, at, :] * (before[x, at, :] - fields[1, x + 1, inner, :])
            for k in (2, 3):
                total = total + weights[4 - k, x, at, :] * (
                    fields[k - 2, x + 1, inner, :] - fields[k, x + 1, inner, :]
                )
            total = total + weights[0, x, at, :] * (
                fields[2, x + 1, inner, :] - last[x, at, :]
            )
            gsum[at, :] = 0.25 * total
        turned = gsum[...].T
        high = turned.astype(BF16)
        lane = pl.ds(pl.multiple_of(x * CY, CY), CY)
        gt[0:NZ, lane] = high
        gt[NZ : 2 * NZ, lane] = (turned - high.astype(F32)).astype(BF16)
        return carry

    lax.fori_loop(0, CX, collect, 0)
    total = jnp.zeros((2 * ROWS, NZ), F32)
    for chunk in range(SLOTS // 256):
        lanes = slice(256 * chunk, 256 * chunk + 256)
        picked = jnp.dot(gt[...], rt[:, lanes], preferred_element_type=F32)
        picked = picked[:NZ] + picked[NZ:]
        index = lax.broadcasted_iota(jnp.int32, (NZ, 256), 0)
        value = jnp.sum(
            jnp.where(index == depth[:, lanes], picked, 0.0), axis=0, keepdims=True
        )
        high = value.astype(BF16).astype(F32)
        low = value - high
        index = lax.broadcasted_iota(jnp.int32, (ROWS, 256), 0)
        mine = index == owner[:, lanes]
        both = jnp.concatenate(
            [jnp.where(mine, high, 0.0), jnp.where(mine, low, 0.0)], axis=0
        ).astype(BF16)
        total = total + lax.dot_general(
            both, bt[:, lanes], (((1,), (1,)), ((), ())), preferred_element_type=F32
        )
    parts[:, 0, :] = total[:ROWS] + total[ROWS:]
    arrived[pl.ds(row, 1)] = parts[pl.ds(row, 1)]
    share(lambda to: parts.at[pl.ds(to, 1)], 1)

    step = adjoint(1)
    inside(step)
    receive(7)
    outside(step)
    second_store = pltpu.make_async_copy(result.at[1], g1_out, store_sem.at[1])
    second_store.start()

    shared(arrived, 3)
    shared(arrived, 2)
    pg_out[...] = jnp.sum(arrived[...], axis=0)[:, 0:SHARE]
    for f in range(8):
        sent(f)
    first_store.wait()
    second_store.wait()


def local(p0, p1, m4, m5, material, speed_sq, admittance, bound_cell, bound_patch):
    block = (CX, CY, NZ)
    anywhere = pl.BlockSpec(memory_space=pl.ANY)
    vmem = pl.BlockSpec(memory_space=pltpu.VMEM)
    return pl.pallas_call(
        kernel,
        out_shape=(
            jax.ShapeDtypeStruct(block, F32),
            jax.ShapeDtypeStruct(block, F32),
            jax.ShapeDtypeStruct((1, SHARE), F32),
        ),
        in_specs=[anywhere] * 5 + [pl.BlockSpec(memory_space=pltpu.SMEM)] + [vmem] * 3,
        out_specs=(anywhere, anywhere, vmem),
        scratch_shapes=[
            pltpu.VMEM((5,) + block, F32),
            pltpu.VMEM(block, jnp.int32),
            pltpu.VMEM((8, PX, PY, NZ), F32),
            pltpu.VMEM(block, F32),
            pltpu.VMEM(block, F32),
            pltpu.VMEM(block, F32),
            pltpu.VMEM(block, F32),
            pltpu.VMEM(block, F32),
            pltpu.VMEM((4,) + block, F32),
            pltpu.VMEM(block, F32),
            pltpu.VMEM((2,) + block, F32),
            pltpu.VMEM((2, CY, NZ), F32),
            pltpu.VMEM((SLOTS, SLOTS), BF16),
            pltpu.VMEM((NZ, SLOTS), BF16),
            pltpu.VMEM((2 * NZ, SLOTS), BF16),
            pltpu.VMEM((2 * NZ, SLOTS), BF16),
            pltpu.VMEM((CY, NZ), F32),
            pltpu.VMEM((1, 1, NZ), F32),
            pltpu.VMEM((ROWS, 1, NZ), F32),
            pltpu.VMEM((ROWS, 1, NZ), F32),
            pltpu.VMEM((ROWS, 1, NZ), F32),
            pltpu.SemaphoreType.DMA((5,)),
            pltpu.SemaphoreType.DMA((2,)),
            pltpu.SemaphoreType.DMA((8, 4)),
            pltpu.SemaphoreType.DMA((8, 4)),
            pltpu.SemaphoreType.DMA((4,)),
        ],
        compiler_params=pltpu.CompilerParams(
            collective_id=0, has_side_effects=True, vmem_limit_bytes=60 << 20
        ),
    )(p0, p1, m4, m5, material, speed_sq, admittance, bound_cell, bound_patch)


def solution(mesh):
    field = P("row", "col", None)
    return jax.shard_map(
        local,
        mesh=mesh,
        in_specs=(field,) * 5 + (P(), P("col", "row"), P("row", "col"), P("row", "col")),
        out_specs=(field, field, P("col", "row")),
        check_vma=False,
    )
```

```python
import jax
import jax.numpy as jnp
from jax import lax
from jax.experimental import pallas as pl
from jax.experimental.pallas import tpu as pltpu
from jax.sharding import PartitionSpec as P

MESH = pl.DeviceIdType.MESH
F32 = jnp.float32
BF16 = jnp.bfloat16
CX, CY, NZ = 16, 128, 128
SLOTS = 2048
ROWS = 32
COLS = 8
SHARE = 64
PX, PY = CX + 2, CY + 16
GROUP = 7
EDGE = 14
PAIR = 7


def natural(step):
    return pl.ds(step, 8, 16)


def along(field, x, count, beside):
    value = field[pl.ds(x, count), 8 : 8 + CY, :].reshape(count * CY, NZ)
    high = value.astype(BF16)
    low = (value - high.astype(F32)).astype(BF16)
    return jnp.dot(
        jnp.concatenate([high, low], axis=1), beside[...], preferred_element_type=F32
    )


def around(field, x, tiles, sums):
    at = lambda plane, t: field[plane, pl.ds(8 + 8 * t, 8), :]
    line = {t: at(x, t) for t in range(tiles[0] - 1, tiles[-1] + 2)}
    found = []
    for t in tiles:
        here = line[t]
        total = (at(x - 1, t) + at(x + 1, t)) + (line[t - 1] + line[t + 1])
        found.append((t, here, total + sums(t) - 6.0 * here))
    return found


def put(field, x, t, value):
    field[x, pl.ds(8 + 8 * t, 8), :] = value
    if t == 15:
        field[x, 1:8, :] = value[0:7]
    if t == 0:
        field[x, CY + 8 : CY + 15, :] = value[1:8]


def kernel(
    p0_in, p1_in, m4_in, m5_in, mat_in, speed, adm, cell, patch,
    g0_out, g1_out, pg_out,
    kinds, raw_p1, raw_p0, raw_m5, raw_m4,
    f0, f1, f2, f3, f4, f5, f6, f7,
    c2, q, before, base0, base1, diff0, diff1, w0, w1, w2, w3, last,
    zs, beside, side, rt, bt, vt, gt, own, table, parts, arrived,
    load_sem, send_sem, recv_sem, share_sem,
):
    fields = (f0, f1, f2, f3, f4, f5, f6, f7)
    bases = (base0, base1)
    diffs = (diff0, diff1)
    weights = (w0, w1, w2, w3)
    row = lax.axis_index("row")
    col = lax.axis_index("col")

    pairs = (
        (p1_in, raw_p1), (mat_in, kinds), (p0_in, raw_p0), (m5_in, raw_m5), (m4_in, raw_m4)
    )
    loads = [
        pltpu.make_async_copy(ref, raw, load_sem.at[n]) for n, (ref, raw) in enumerate(pairs)
    ]
    for load in loads:
        load.start()

    barrier = pltpu.get_barrier_semaphore()

    def greet(step, carry):
        pl.semaphore_signal(
            barrier, inc=1, device_id=(lax.rem(row + step, ROWS), col), device_id_type=MESH
        )
        return carry

    lax.fori_loop(1, ROWS, greet, 0)
    for step in (1, COLS - 1):
        pl.semaphore_signal(
            barrier, inc=1, device_id=(row, lax.rem(col + step, COLS)), device_id_type=MESH
        )

    zero_plane = jnp.zeros((CY, NZ), F32)
    zero_row = jnp.zeros((CX, 1, NZ), F32)

    @pl.when(row == 0)
    def _():
        for f in range(8):
            fields[f][0, 8 : 8 + CY, :] = zero_plane

    @pl.when(row == ROWS - 1)
    def _():
        for f in range(8):
            fields[f][PX - 1, 8 : 8 + CY, :] = zero_plane

    @pl.when(col == 0)
    def _():
        for f in range(8):
            fields[f][1 : 1 + CX, 0:1, :] = zero_row

    @pl.when(col == COLS - 1)
    def _():
        for f in range(8):
            fields[f][1 : 1 + CX, PY - 1 : PY, :] = zero_row

    own[...] = jnp.zeros_like(own)
    own[0, :, 0:SHARE] = adm[...]
    table[pl.ds(row, 1)] = own[...]

    pl.semaphore_wait(barrier, ROWS + 1)

    sides = (
        (row < ROWS - 1, (row + 1, col)),
        (row > 0, (row - 1, col)),
        (col < COLS - 1, (row, col + 1)),
        (col > 0, (row, col - 1)),
    )
    comes = (row > 0, row < ROWS - 1, col > 0, col < COLS - 1)

    def copies(f):
        field = fields[f]
        pairs = (
            (field.at[CX, 8 : 8 + CY, :], field.at[0, 8 : 8 + CY, :]),
            (field.at[1, 8 : 8 + CY, :], field.at[PX - 1, 8 : 8 + CY, :]),
            (field.at[1 : 1 + CX, CY + 7 : CY + 8, :], field.at[1 : 1 + CX, 0:1, :]),
            (field.at[1 : 1 + CX, 8:9, :], field.at[1 : 1 + CX, PY - 1 : PY, :]),
        )
        if f == 0:
            pairs = (
                (p1_in.at[CX - 1], side.at[0]),
                (p1_in.at[0], side.at[1]),
                (p1_in.at[:, CY - 1 : CY, :], pairs[2][1]),
                (p1_in.at[:, 0:1, :], pairs[3][1]),
            )
        return [
            pltpu.make_async_remote_copy(
                src, dst, send_sem.at[f, d], recv_sem.at[f, d],
                device_id=sides[d][1], device_id_type=MESH,
            )
            for d, (src, dst) in enumerate(pairs)
        ]

    def send(f):
        for d, copy in enumerate(copies(f)):
            pl.when(sides[d][0])(copy.start)

    def receive(f):
        for d, copy in enumerate(copies(f)):
            pl.when(comes[d])(copy.wait_recv)

    def sent(f):
        for d, copy in enumerate(copies(f)):
            pl.when(sides[d][0])(copy.wait_send)

    send(0)

    def share(source, sem):
        def start(step, carry):
            to = lax.rem(row + step, ROWS)
            pltpu.make_async_remote_copy(
                source(to), (table if sem == 0 else arrived).at[pl.ds(row, 1)],
                share_sem.at[2 * sem], share_sem.at[2 * sem + 1],
                device_id=(to, col), device_id_type=MESH,
            ).start()
            return carry

        lax.fori_loop(1, ROWS, start, 0)

    def shared(buffer, which):
        rest = buffer.at[pl.ds(0, ROWS - 1)]
        pltpu.make_async_copy(rest, rest, share_sem.at[which]).wait()

    share(lambda to: own, 0)

    cells = cell[...]
    spots = patch[...]
    depth = cells & (NZ - 1)
    y = (cells >> 7) & (CY - 1)
    line = (cells >> 14) * CY + (y & 15) * 8 + (y >> 4)
    owner = spots >> 6
    place = spots & (SHARE - 1)

    def build(block, carry):
        start = pl.multiple_of(block * 16, 16)
        index = lax.broadcasted_iota(jnp.int32, (16, SLOTS), 0) + start
        rt[pl.ds(start, 16), :] = jnp.where(index == line, 1.0, 0.0).astype(BF16)
        return carry

    lax.fori_loop(0, SLOTS // 16, build, 0)
    index = lax.broadcasted_iota(jnp.int32, (2 * NZ, NZ), 0) & (NZ - 1)
    apart = index - lax.broadcasted_iota(jnp.int32, (2 * NZ, NZ), 1)
    beside[...] = jnp.where((apart == 1) | (apart == -1), 1.0, 0.0).astype(BF16)
    index = lax.broadcasted_iota(jnp.int32, (NZ, SLOTS), 0)
    bt[...] = jnp.where(index == place, 1.0, 0.0).astype(BF16)

    loads[0].wait()
    loads[1].wait()
    speeds = [speed[n] for n in range(8)]

    def arrange(x, carry):
        values = [raw_p1[x, natural(t), :] for t in range(16)]
        sorts = [kinds[x, natural(t), :] for t in range(16)]
        for t in range(16):
            put(f0, x + 1, t, values[t])
        for t in range(16):
            value = jnp.full((8, NZ), speeds[0], F32)
            for n in range(1, 8):
                value = jnp.where(sorts[t] == n, speeds[n], value)
            c2[x, pl.ds(8 * t, 8), :] = value
        return carry

    lax.fori_loop(0, CX, arrange, 0)

    loads[2].wait()
    loads[3].wait()
    loads[4].wait()

    def arrange_rest(x, carry):
        values = [raw_p0[x, natural(t), :] for t in range(16)]
        for t in range(16):
            before[x, pl.ds(8 * t, 8), :] = values[t]
        return carry

    lax.fori_loop(0, CX, arrange_rest, 0)

    shared(table, 1)
    shared(table, 0)
    strip = 0.25 * table[:, 0, :]
    strip_high = strip.astype(BF16)
    strip_low = (strip - strip_high.astype(F32)).astype(BF16)
    found = jnp.dot(
        jnp.concatenate([strip_high, strip_low], axis=0), bt[...], preferred_element_type=F32
    )
    found = found[:ROWS] + found[ROWS:]
    index = lax.broadcasted_iota(jnp.int32, (ROWS, SLOTS), 0)
    slot = jnp.sum(jnp.where(index == owner, found, 0.0), axis=0, keepdims=True)
    slot_high = slot.astype(BF16).astype(F32)
    slot_low = slot - slot_high
    index = lax.broadcasted_iota(jnp.int32, (NZ, SLOTS), 0)
    vt[0:NZ, :] = jnp.where(index == depth, slot_high, 0.0).astype(BF16)
    vt[NZ : 2 * NZ, :] = jnp.where(index == depth, slot_low, 0.0).astype(BF16)

    def spread(pair, carry):
        start = pl.multiple_of(pair * 256, 256)
        both = lax.dot_general(
            rt[pl.ds(start, 256), :], vt[...], (((1,), (1,)), ((), ())), preferred_element_type=F32
        )
        for half in range(2):
            x = 2 * pair + half
            for t in range(16):
                at = half * CY + 8 * t
                gamma = both[at : at + 8, 0:NZ] + both[at : at + 8, NZ : 2 * NZ]
                here = pl.ds(8 * t, 8)
                scale = 1.0 / (1.0 + gamma)
                high = raw_m5[x, natural(t), :]
                low = raw_m4[x, natural(t), :]
                weight = scale * high
                twice = 2.0 * weight
                q[x, here, :] = scale
                w0[x, here, :] = weight
                put(f4, x + 1, t, c2[x, here, :] * weight)
                base0[x, here, :] = low + twice
                diff0[x, here, :] = high - twice
        return carry

    lax.fori_loop(0, CX // 2, spread, 0, unroll=4)
    send(4)

    def forward(k):
        def group(work):
            found = []
            for x, tiles, sums in work:
                for t, here, change in around(fields[k - 1], x, tiles, sums):
                    at = pl.ds(8 * t, 8)
                    if k == 1:
                        old = before[x - 1, at, :]
                    else:
                        old = fields[k - 2][x, pl.ds(8 + 8 * t, 8), :]
                    new = old + q[x - 1, at, :] * (2.0 * (here - old) + c2[x - 1, at, :] * change)
                    found.append((x, t, new))
            for x, t, new in found:
                if k == 4:
                    last[x - 1, pl.ds(8 * t, 8), :] = new
                else:
                    put(fields[k], x, t, new)

        return fields[k - 1], group

    def adjoint(k):
        f = 8 - k
        base, next_base = bases[k % 2], bases[1 - k % 2]
        diff, next_diff = diffs[k % 2], diffs[1 - k % 2]

        def group(work):
            found = []
            for x, tiles, sums in work:
                for t, here, change in around(fields[f], x, tiles, sums):
                    at = pl.ds(8 * t, 8)
                    high = base[x - 1, at, :] + change
                    if k == 1:
                        found.append((x, t, high))
                        continue
                    weight = q[x - 1, at, :] * high
                    twice = 2.0 * weight
                    found.append(
                        (x, t, weight, c2[x - 1, at, :] * weight,
                         diff[x - 1, at, :] + twice, high - twice)
                    )
            for x, t, *values in found:
                at = pl.ds(8 * t, 8)
                if k == 1:
                    g1_out[x - 1, natural(t), :] = values[0]
                    continue
                weights[f - 3][x - 1, at, :] = values[0]
                put(fields[f + 1], x, t, values[1])
                next_base[x - 1, at, :] = values[2]
                if k == 2:
                    g0_out[x - 1, natural(t), :] = values[3]
                else:
                    next_diff[x - 1, at, :] = values[3]

        return fields[f], group

    def inside(step):
        field, group = step

        def body(n, carry):
            x = 2 + PAIR * n
            sums = along(field, x, PAIR, beside)
            for i in range(PAIR):
                tile = lambda t, i=i: sums[CY * i + 8 * t : CY * i + 8 * t + 8]
                for t in (0, 15):
                    zs[x + i - 1, pl.ds(8 * t, 8), :] = tile(t)
                for start in range(1, 15, GROUP):
                    group([(x + i, range(start, start + GROUP), tile)])
            return carry

        for x in (1, CX):
            zs[x - 1] = along(field, x, 1, beside)
        lax.fori_loop(0, 14 // PAIR, body, 0)

    def outside(step):
        field, group = step

        def tile(x):
            return lambda t: zs[x - 1, pl.ds(8 * t, 8), :]

        def ends(n, carry):
            x = 1 + n * (CX - 1)
            for start in range(0, 16, 8):
                group([(x, range(start, start + 8), tile(x))])
            return carry

        def edges(n, carry):
            x = 2 + EDGE * n
            for t in (0, 15):
                group([(x + i, (t,), tile(x + i)) for i in range(EDGE)])
            return carry

        lax.fori_loop(0, 2, ends, 0)
        lax.fori_loop(0, 14 // EDGE, edges, 0)

    inside(forward(1))
    receive(0)
    for n, plane, there in ((0, 0, comes[0]), (1, PX - 1, comes[1])):
        def place_side(n=n, plane=plane):
            for t in range(16):
                f0[plane, pl.ds(8 + 8 * t, 8), :] = side[n, natural(t), :]

        pl.when(there)(place_side)
    outside(forward(1))
    send(1)

    for k in (2, 3, 4):
        level = 6 - k
        step = adjoint(level)
        inside(step)
        receive(8 - level)
        outside(step)
        send(9 - level)
        step = forward(k)
        inside(step)
        receive(k - 1)
        outside(step)
        if k < 4:
            send(k)

    def collect(x, carry):
        tiles = []
        for t in range(16):
            at = pl.ds(8 * t, 8)
            inner = pl.ds(8 + 8 * t, 8)
            states = [before[x, at, :]]
            states += [fields[k][x + 1, inner, :] for k in range(4)]
            states.append(last[x, at, :])
            total = w3[x, at, :] * (states[0] - states[2])
            for k in (2, 3, 4):
                total = total + weights[4 - k][x, at, :] * (states[k - 1] - states[k + 1])
            tiles.append(0.25 * total)
        turned = jnp.concatenate(tiles, axis=0).T
        high = turned.astype(BF16)
        lane = pl.ds(pl.multiple_of(x * CY, CY), CY)
        gt[0:NZ, lane] = high
        gt[NZ : 2 * NZ, lane] = (turned - high.astype(F32)).astype(BF16)
        return carry

    lax.fori_loop(0, CX, collect, 0, unroll=4)
    total = jnp.zeros((2 * ROWS, NZ), F32)
    for chunk in range(SLOTS // 256):
        lanes = slice(256 * chunk, 256 * chunk + 256)
        picked = jnp.dot(gt[...], rt[:, lanes], preferred_element_type=F32)
        picked = picked[:NZ] + picked[NZ:]
        index = lax.broadcasted_iota(jnp.int32, (NZ, 256), 0)
        value = jnp.sum(
            jnp.where(index == depth[:, lanes], picked, 0.0), axis=0, keepdims=True
        )
        high = value.astype(BF16).astype(F32)
        low = value - high
        index = lax.broadcasted_iota(jnp.int32, (ROWS, 256), 0)
        mine = index == owner[:, lanes]
        both = jnp.concatenate(
            [jnp.where(mine, high, 0.0), jnp.where(mine, low, 0.0)], axis=0
        ).astype(BF16)
        total = total + lax.dot_general(
            both, bt[:, lanes], (((1,), (1,)), ((), ())), preferred_element_type=F32
        )
    parts[:, 0, :] = total[:ROWS] + total[ROWS:]
    arrived[pl.ds(row, 1)] = parts[pl.ds(row, 1)]
    share(lambda to: parts.at[pl.ds(to, 1)], 1)

    step = adjoint(1)
    inside(step)
    receive(7)
    outside(step)

    shared(arrived, 3)
    shared(arrived, 2)
    pg_out[...] = jnp.sum(arrived[...], axis=0)[:, 0:SHARE]
    for f in range(8):
        sent(f)


def hand_over(g0_in, g1_in, pg_in, g0_out, g1_out, pg_out, sem):
    pairs = ((g0_in, g0_out), (g1_in, g1_out), (pg_in, pg_out))
    copies = [pltpu.make_async_copy(src, dst, sem.at[n]) for n, (src, dst) in enumerate(pairs)]
    for copy in copies:
        copy.start()
    for copy in copies:
        copy.wait()


def local(p0, p1, m4, m5, material, speed_sq, admittance, bound_cell, bound_patch):
    block = (CX, CY, NZ)
    anywhere = pl.BlockSpec(memory_space=pl.ANY)
    far = pl.BlockSpec(memory_space=pltpu.HBM)
    vmem = pl.BlockSpec(memory_space=pltpu.VMEM)
    shapes = (
        jax.ShapeDtypeStruct(block, F32),
        jax.ShapeDtypeStruct(block, F32),
        jax.ShapeDtypeStruct((1, SHARE), F32),
    )
    results = pl.pallas_call(
        kernel,
        out_shape=shapes,
        in_specs=[far] * 5 + [pl.BlockSpec(memory_space=pltpu.SMEM)] + [vmem] * 3,
        out_specs=(vmem,) * 3,
        scratch_shapes=[pltpu.VMEM(block, jnp.int32)]
        + [pltpu.VMEM(block, F32)] * 4
        + [pltpu.VMEM((PX, PY, NZ), F32)] * 8
        + [pltpu.VMEM(block, F32)] * 12
        + [
            pltpu.VMEM(block, F32),
            pltpu.VMEM((2 * NZ, NZ), BF16),
            pltpu.VMEM((2, CY, NZ), F32),
            pltpu.VMEM((SLOTS, SLOTS), BF16),
            pltpu.VMEM((NZ, SLOTS), BF16),
            pltpu.VMEM((2 * NZ, SLOTS), BF16),
            pltpu.VMEM((2 * NZ, SLOTS), BF16),
            pltpu.VMEM((1, 1, NZ), F32),
            pltpu.VMEM((ROWS, 1, NZ), F32),
            pltpu.VMEM((ROWS, 1, NZ), F32),
            pltpu.VMEM((ROWS, 1, NZ), F32),
            pltpu.SemaphoreType.DMA((5,)),
            pltpu.SemaphoreType.DMA((8, 4)),
            pltpu.SemaphoreType.DMA((8, 4)),
            pltpu.SemaphoreType.DMA((4,)),
        ],
        compiler_params=pltpu.CompilerParams(
            collective_id=0, has_side_effects=True, vmem_limit_bytes=48 << 20
        ),
    )(p0, p1, m4, m5, material, speed_sq, admittance, bound_cell, bound_patch)
    return pl.pallas_call(
        hand_over,
        out_shape=shapes,
        in_specs=[vmem] * 3,
        out_specs=(anywhere,) * 3,
        scratch_shapes=[pltpu.SemaphoreType.DMA((3,))],
        compiler_params=pltpu.CompilerParams(vmem_limit_bytes=4 << 20),
    )(*results)


def solution(mesh):
    field = P("row", "col", None)
    return jax.shard_map(
        local,
        mesh=mesh,
        in_specs=(field,) * 5 + (P(), P("col", "row"), P("row", "col"), P("row", "col")),
        out_specs=(field, field, P("col", "row")),
        check_vma=False,
    )
```

```python
import jax
import jax.numpy as jnp
from jax import lax
from jax.experimental import pallas as pl
from jax.experimental.pallas import tpu as pltpu
from jax.sharding import PartitionSpec as P

MESH = pl.DeviceIdType.MESH
F32 = jnp.float32
BF16 = jnp.bfloat16
CX, CY, NZ = 16, 128, 128
SLOTS = 2048
ROWS = 32
COLS = 8
SHARE = 64
PX, PY = CX + 2, CY + 16
GROUP = 7
EDGE = 14
PAIR = 7
RIM = 512


def natural(step):
    return pl.ds(step, 8, 16)


def along(field, x, count, beside):
    value = field[pl.ds(x, count), 8 : 8 + CY, :].reshape(count * CY, NZ)
    high = value.astype(BF16)
    low = (value - high.astype(F32)).astype(BF16)
    return jnp.dot(
        jnp.concatenate([high, low], axis=1), beside[...], preferred_element_type=F32
    )


def around(field, x, tiles, sums):
    at = lambda plane, t: field[plane, pl.ds(8 + 8 * t, 8), :]
    line = {t: at(x, t) for t in range(tiles[0] - 1, tiles[-1] + 2)}
    found = []
    for t in tiles:
        here = line[t]
        total = (at(x - 1, t) + at(x + 1, t)) + (line[t - 1] + line[t + 1])
        found.append((t, here, total + sums(t) - 6.0 * here))
    return found


def put(field, x, t, value):
    field[x, pl.ds(8 + 8 * t, 8), :] = value
    if t == 15:
        field[x, 1:8, :] = value[0:7]
    if t == 0:
        field[x, CY + 8 : CY + 15, :] = value[1:8]


def kernel(
    p0_in, p1_in, m4_in, m5_in, mat_in, speed, adm, cell, patch,
    g0_out, g1_out, pg_out,
    kinds, raw_p1, raw_p0, raw_m5, raw_m4,
    f0, f1, f2, f3, f4, f5, f6, f7,
    c2, q, before, base0, base1, diff0, diff1, w0, w1, w2, w3, last,
    zs, beside, side, rt, bt, vt, gt, rt_rim, gt_rim, own, table, parts, arrived,
    load_sem, send_sem, recv_sem, share_sem,
):
    fields = (f0, f1, f2, f3, f4, f5, f6, f7)
    bases = (base0, base1)
    diffs = (diff0, diff1)
    weights = (w0, w1, w2, w3)
    row = lax.axis_index("row")
    col = lax.axis_index("col")

    pairs = (
        (p1_in, raw_p1), (mat_in, kinds), (p0_in, raw_p0), (m5_in, raw_m5), (m4_in, raw_m4)
    )
    loads = [
        pltpu.make_async_copy(ref, raw, load_sem.at[n]) for n, (ref, raw) in enumerate(pairs)
    ]
    for load in loads:
        load.start()

    barrier = pltpu.get_barrier_semaphore()

    def greet(step, carry):
        pl.semaphore_signal(
            barrier, inc=1, device_id=(lax.rem(row + step, ROWS), col), device_id_type=MESH
        )
        return carry

    lax.fori_loop(1, ROWS, greet, 0)
    for step in (1, COLS - 1):
        pl.semaphore_signal(
            barrier, inc=1, device_id=(row, lax.rem(col + step, COLS)), device_id_type=MESH
        )

    zero_plane = jnp.zeros((CY, NZ), F32)
    zero_row = jnp.zeros((CX, 1, NZ), F32)

    @pl.when(row == 0)
    def _():
        for f in range(8):
            fields[f][0, 8 : 8 + CY, :] = zero_plane

    @pl.when(row == ROWS - 1)
    def _():
        for f in range(8):
            fields[f][PX - 1, 8 : 8 + CY, :] = zero_plane

    @pl.when(col == 0)
    def _():
        for f in range(8):
            fields[f][1 : 1 + CX, 0:1, :] = zero_row

    @pl.when(col == COLS - 1)
    def _():
        for f in range(8):
            fields[f][1 : 1 + CX, PY - 1 : PY, :] = zero_row

    own[...] = jnp.zeros_like(own)
    own[0, :, 0:SHARE] = adm[...]
    table[pl.ds(row, 1)] = own[...]

    pl.semaphore_wait(barrier, ROWS + 1)

    sides = (
        (row < ROWS - 1, (row + 1, col)),
        (row > 0, (row - 1, col)),
        (col < COLS - 1, (row, col + 1)),
        (col > 0, (row, col - 1)),
    )
    comes = (row > 0, row < ROWS - 1, col > 0, col < COLS - 1)

    def copies(f):
        field = fields[f]
        pairs = (
            (field.at[CX, 8 : 8 + CY, :], field.at[0, 8 : 8 + CY, :]),
            (field.at[1, 8 : 8 + CY, :], field.at[PX - 1, 8 : 8 + CY, :]),
            (field.at[1 : 1 + CX, CY + 7 : CY + 8, :], field.at[1 : 1 + CX, 0:1, :]),
            (field.at[1 : 1 + CX, 8:9, :], field.at[1 : 1 + CX, PY - 1 : PY, :]),
        )
        if f == 0:
            pairs = (
                (p1_in.at[CX - 1], side.at[0]),
                (p1_in.at[0], side.at[1]),
                (p1_in.at[:, CY - 1 : CY, :], pairs[2][1]),
                (p1_in.at[:, 0:1, :], pairs[3][1]),
            )
        return [
            pltpu.make_async_remote_copy(
                src, dst, send_sem.at[f, d], recv_sem.at[f, d],
                device_id=sides[d][1], device_id_type=MESH,
            )
            for d, (src, dst) in enumerate(pairs)
        ]

    def send(f):
        for d, copy in enumerate(copies(f)):
            pl.when(sides[d][0])(copy.start)

    def receive(f):
        for d, copy in enumerate(copies(f)):
            pl.when(comes[d])(copy.wait_recv)

    def sent(f):
        for d, copy in enumerate(copies(f)):
            pl.when(sides[d][0])(copy.wait_send)

    send(0)

    def share(source, sem):
        def start(step, carry):
            to = lax.rem(row + step, ROWS)
            pltpu.make_async_remote_copy(
                source(to), (table if sem == 0 else arrived).at[pl.ds(row, 1)],
                share_sem.at[2 * sem], share_sem.at[2 * sem + 1],
                device_id=(to, col), device_id_type=MESH,
            ).start()
            return carry

        lax.fori_loop(1, ROWS, start, 0)

    def shared(buffer, which):
        rest = buffer.at[pl.ds(0, ROWS - 1)]
        pltpu.make_async_copy(rest, rest, share_sem.at[which]).wait()

    share(lambda to: own, 0)

    cells = cell[...]
    spots = patch[...]
    depth = cells & (NZ - 1)
    y = (cells >> 7) & (CY - 1)
    line = (cells >> 14) * CY + (y & 15) * 8 + (y >> 4)
    owner = spots >> 6
    place = spots & (SHARE - 1)

    def build(block, carry):
        start = pl.multiple_of(block * 16, 16)
        index = lax.broadcasted_iota(jnp.int32, (16, SLOTS), 0) + start
        rt[pl.ds(start, 16), :] = jnp.where(index == line, 1.0, 0.0).astype(BF16)
        return carry

    lax.fori_loop(0, SLOTS // 16, build, 0)
    plane = cells >> 14
    inner = jnp.where((y & 15) == 0, 256, 384) + 8 * (plane - 1) + (y >> 4)
    inner = jnp.where(((y & 15) == 0) | ((y & 15) == 15), inner, -1)
    ends_line = jnp.where(plane == 0, line, line - (CX - 2) * CY)
    rim = jnp.where((plane == 0) | (plane == CX - 1), ends_line, inner)
    rim = jnp.where(cells < 0, -1, rim)

    def build_rim(block, carry):
        start = pl.multiple_of(block * 16, 16)
        index = lax.broadcasted_iota(jnp.int32, (16, SLOTS), 0) + start
        rt_rim[pl.ds(start, 16), :] = jnp.where(index == rim, 1.0, 0.0).astype(BF16)
        return carry

    lax.fori_loop(0, RIM // 16, build_rim, 0)
    index = lax.broadcasted_iota(jnp.int32, (2 * NZ, NZ), 0) & (NZ - 1)
    apart = index - lax.broadcasted_iota(jnp.int32, (2 * NZ, NZ), 1)
    beside[...] = jnp.where((apart == 1) | (apart == -1), 1.0, 0.0).astype(BF16)
    index = lax.broadcasted_iota(jnp.int32, (NZ, SLOTS), 0)
    bt[...] = jnp.where(index == place, 1.0, 0.0).astype(BF16)

    loads[0].wait()
    loads[1].wait()
    speeds = [speed[n] for n in range(8)]

    def arrange(x, carry):
        values = [raw_p1[x, natural(t), :] for t in range(16)]
        sorts = [kinds[x, natural(t), :] for t in range(16)]
        for t in range(16):
            put(f0, x + 1, t, values[t])
        for t in range(16):
            value = jnp.full((8, NZ), speeds[0], F32)
            for n in range(1, 8):
                value = jnp.where(sorts[t] == n, speeds[n], value)
            c2[x, pl.ds(8 * t, 8), :] = value
        return carry

    lax.fori_loop(0, CX, arrange, 0)

    loads[2].wait()
    loads[3].wait()
    loads[4].wait()

    def arrange_rest(x, carry):
        values = [raw_p0[x, natural(t), :] for t in range(16)]
        for t in range(16):
            before[x, pl.ds(8 * t, 8), :] = values[t]
        return carry

    lax.fori_loop(0, CX, arrange_rest, 0)

    shared(table, 1)
    shared(table, 0)
    strip = 0.25 * table[:, 0, :]
    strip_high = strip.astype(BF16)
    strip_low = (strip - strip_high.astype(F32)).astype(BF16)
    found = jnp.dot(
        jnp.concatenate([strip_high, strip_low], axis=0), bt[...], preferred_element_type=F32
    )
    found = found[:ROWS] + found[ROWS:]
    index = lax.broadcasted_iota(jnp.int32, (ROWS, SLOTS), 0)
    slot = jnp.sum(jnp.where(index == owner, found, 0.0), axis=0, keepdims=True)
    slot_high = slot.astype(BF16).astype(F32)
    slot_low = slot - slot_high
    index = lax.broadcasted_iota(jnp.int32, (NZ, SLOTS), 0)
    vt[0:NZ, :] = jnp.where(index == depth, slot_high, 0.0).astype(BF16)
    vt[NZ : 2 * NZ, :] = jnp.where(index == depth, slot_low, 0.0).astype(BF16)

    def spread(pair, carry):
        start = pl.multiple_of(pair * 256, 256)
        both = lax.dot_general(
            rt[pl.ds(start, 256), :], vt[...], (((1,), (1,)), ((), ())), preferred_element_type=F32
        )
        for half in range(2):
            x = 2 * pair + half
            for t in range(16):
                at = half * CY + 8 * t
                gamma = both[at : at + 8, 0:NZ] + both[at : at + 8, NZ : 2 * NZ]
                here = pl.ds(8 * t, 8)
                scale = 1.0 / (1.0 + gamma)
                high = raw_m5[x, natural(t), :]
                low = raw_m4[x, natural(t), :]
                weight = scale * high
                twice = 2.0 * weight
                q[x, here, :] = scale
                w0[x, here, :] = weight
                put(f4, x + 1, t, c2[x, here, :] * weight)
                base0[x, here, :] = low + twice
                diff0[x, here, :] = high - twice
        return carry

    lax.fori_loop(0, CX // 2, spread, 0, unroll=4)
    send(4)

    def forward(k):
        def group(work):
            found = []
            for x, tiles, sums in work:
                for t, here, change in around(fields[k - 1], x, tiles, sums):
                    at = pl.ds(8 * t, 8)
                    if k == 1:
                        old = before[x - 1, at, :]
                    else:
                        old = fields[k - 2][x, pl.ds(8 + 8 * t, 8), :]
                    new = old + q[x - 1, at, :] * (2.0 * (here - old) + c2[x - 1, at, :] * change)
                    found.append((x, t, new))
            for x, t, new in found:
                if k == 4:
                    last[x - 1, pl.ds(8 * t, 8), :] = new
                else:
                    put(fields[k], x, t, new)

        return fields[k - 1], group

    def adjoint(k):
        f = 8 - k
        base, next_base = bases[k % 2], bases[1 - k % 2]
        diff, next_diff = diffs[k % 2], diffs[1 - k % 2]

        def group(work):
            found = []
            for x, tiles, sums in work:
                for t, here, change in around(fields[f], x, tiles, sums):
                    at = pl.ds(8 * t, 8)
                    high = base[x - 1, at, :] + change
                    if k == 1:
                        found.append((x, t, high))
                        continue
                    weight = q[x - 1, at, :] * high
                    twice = 2.0 * weight
                    found.append(
                        (x, t, weight, c2[x - 1, at, :] * weight,
                         diff[x - 1, at, :] + twice, high - twice)
                    )
            for x, t, *values in found:
                at = pl.ds(8 * t, 8)
                if k == 1:
                    g1_out[x - 1, natural(t), :] = values[0]
                    continue
                weights[f - 3][x - 1, at, :] = values[0]
                put(fields[f + 1], x, t, values[1])
                next_base[x - 1, at, :] = values[2]
                if k == 2:
                    g0_out[x - 1, natural(t), :] = values[3]
                else:
                    next_diff[x - 1, at, :] = values[3]

        return fields[f], group

    def inside(step):
        field, group = step

        def body(n, carry):
            x = 2 + PAIR * n
            sums = along(field, x, PAIR, beside)
            for i in range(PAIR):
                tile = lambda t, i=i: sums[CY * i + 8 * t : CY * i + 8 * t + 8]
                for t in (0, 15):
                    zs[x + i - 1, pl.ds(8 * t, 8), :] = tile(t)
                for start in range(1, 15, GROUP):
                    group([(x + i, range(start, start + GROUP), tile)])
            return carry

        for x in (1, CX):
            zs[x - 1] = along(field, x, 1, beside)
        lax.fori_loop(0, 14 // PAIR, body, 0)

    def outside(step):
        field, group = step

        def tile(x):
            return lambda t: zs[x - 1, pl.ds(8 * t, 8), :]

        def ends(n, carry):
            x = 1 + n * (CX - 1)
            for start in range(0, 16, 8):
                group([(x, range(start, start + 8), tile(x))])
            return carry

        def edges(n, carry):
            x = 2 + EDGE * n
            for t in (0, 15):
                group([(x + i, (t,), tile(x + i)) for i in range(EDGE)])
            return carry

        lax.fori_loop(0, 2, ends, 0)
        lax.fori_loop(0, 14 // EDGE, edges, 0)

    inside(forward(1))
    receive(0)
    for n, plane, there in ((0, 0, comes[0]), (1, PX - 1, comes[1])):
        def place_side(n=n, plane=plane):
            for t in range(16):
                f0[plane, pl.ds(8 + 8 * t, 8), :] = side[n, natural(t), :]

        pl.when(there)(place_side)
    outside(forward(1))
    send(1)

    for k in (2, 3):
        level = 6 - k
        step = adjoint(level)
        inside(step)
        receive(8 - level)
        outside(step)
        send(9 - level)
        step = forward(k)
        inside(step)
        receive(k - 1)
        outside(step)
        send(k)

    def product(x, t):
        at = pl.ds(8 * t, 8)
        inner = pl.ds(8 + 8 * t, 8)
        states = [before[x, at, :]]
        states += [fields[k][x + 1, inner, :] for k in range(4)]
        states.append(last[x, at, :])
        total = w3[x, at, :] * (states[0] - states[2])
        for k in (2, 3, 4):
            total = total + weights[4 - k][x, at, :] * (states[k - 1] - states[k + 1])
        return 0.25 * total

    def turn(target, lane, tiles):
        turned = jnp.concatenate(tiles, axis=0).T
        high = turned.astype(BF16)
        target[0:NZ, lane] = high
        target[NZ : 2 * NZ, lane] = (turned - high.astype(F32)).astype(BF16)

    def collect(x, carry):
        none = jnp.zeros((8, NZ), F32)
        tiles = [none] + [product(x, t) for t in range(1, 15)] + [none]
        turn(gt, pl.ds(pl.multiple_of(x * CY, CY), CY), tiles)
        return carry

    def pick(source, start, stop, table_of_rows, lanes):
        picked = jnp.dot(
            source[:, start:stop], table_of_rows[start:stop, lanes], preferred_element_type=F32
        )
        picked = picked[:NZ] + picked[NZ:]
        index = lax.broadcasted_iota(jnp.int32, (NZ, 256), 0)
        return jnp.sum(
            jnp.where(index == depth[:, lanes], picked, 0.0), axis=0, keepdims=True
        )

    step = adjoint(2)
    ahead = forward(4)
    inside(step)
    receive(6)
    outside(step)
    send(7)
    inside(ahead)
    lax.fori_loop(1, CX - 1, collect, 0, unroll=2)
    early = [
        pick(gt, CY, (CX - 1) * CY, rt, slice(256 * c, 256 * c + 256))
        for c in range(SLOTS // 256)
    ]
    receive(3)
    outside(ahead)
    none = jnp.zeros((8, NZ), F32)
    turn(gt_rim, slice(0, CY), [product(0, t) for t in range(16)])
    turn(gt_rim, slice(CY, 2 * CY), [product(CX - 1, t) for t in range(16)])
    for n, t in ((2, 0), (3, 15)):
        tiles = [product(x, t) for x in range(1, CX - 1)] + [none, none]
        turn(gt_rim, slice(n * CY, (n + 1) * CY), tiles)
    total = jnp.zeros((2 * ROWS, NZ), F32)
    for chunk in range(SLOTS // 256):
        lanes = slice(256 * chunk, 256 * chunk + 256)
        value = early[chunk] + pick(gt_rim, 0, RIM, rt_rim, lanes)
        high = value.astype(BF16).astype(F32)
        low = value - high
        index = lax.broadcasted_iota(jnp.int32, (ROWS, 256), 0)
        mine = index == owner[:, lanes]
        both = jnp.concatenate(
            [jnp.where(mine, high, 0.0), jnp.where(mine, low, 0.0)], axis=0
        ).astype(BF16)
        total = total + lax.dot_general(
            both, bt[:, lanes], (((1,), (1,)), ((), ())), preferred_element_type=F32
        )
    parts[:, 0, :] = total[:ROWS] + total[ROWS:]
    arrived[pl.ds(row, 1)] = parts[pl.ds(row, 1)]
    share(lambda to: parts.at[pl.ds(to, 1)], 1)

    step = adjoint(1)
    inside(step)
    receive(7)
    outside(step)

    shared(arrived, 3)
    shared(arrived, 2)
    pg_out[...] = jnp.sum(arrived[...], axis=0)[:, 0:SHARE]
    for f in range(8):
        sent(f)


def hand_over(g0_in, g1_in, pg_in, g0_out, g1_out, pg_out, sem):
    pairs = ((g0_in, g0_out), (g1_in, g1_out), (pg_in, pg_out))
    copies = [pltpu.make_async_copy(src, dst, sem.at[n]) for n, (src, dst) in enumerate(pairs)]
    for copy in copies:
        copy.start()
    for copy in copies:
        copy.wait()


def local(p0, p1, m4, m5, material, speed_sq, admittance, bound_cell, bound_patch):
    block = (CX, CY, NZ)
    anywhere = pl.BlockSpec(memory_space=pl.ANY)
    far = pl.BlockSpec(memory_space=pltpu.HBM)
    vmem = pl.BlockSpec(memory_space=pltpu.VMEM)
    shapes = (
        jax.ShapeDtypeStruct(block, F32),
        jax.ShapeDtypeStruct(block, F32),
        jax.ShapeDtypeStruct((1, SHARE), F32),
    )
    results = pl.pallas_call(
        kernel,
        out_shape=shapes,
        in_specs=[far] * 5 + [pl.BlockSpec(memory_space=pltpu.SMEM)] + [vmem] * 3,
        out_specs=(vmem,) * 3,
        scratch_shapes=[pltpu.VMEM(block, jnp.int32)]
        + [pltpu.VMEM(block, F32)] * 4
        + [pltpu.VMEM((PX, PY, NZ), F32)] * 8
        + [pltpu.VMEM(block, F32)] * 12
        + [
            pltpu.VMEM(block, F32),
            pltpu.VMEM((2 * NZ, NZ), BF16),
            pltpu.VMEM((2, CY, NZ), F32),
            pltpu.VMEM((SLOTS, SLOTS), BF16),
            pltpu.VMEM((NZ, SLOTS), BF16),
            pltpu.VMEM((2 * NZ, SLOTS), BF16),
            pltpu.VMEM((2 * NZ, SLOTS), BF16),
            pltpu.VMEM((RIM, SLOTS), BF16),
            pltpu.VMEM((2 * NZ, RIM), BF16),
            pltpu.VMEM((1, 1, NZ), F32),
            pltpu.VMEM((ROWS, 1, NZ), F32),
            pltpu.VMEM((ROWS, 1, NZ), F32),
            pltpu.VMEM((ROWS, 1, NZ), F32),
            pltpu.SemaphoreType.DMA((5,)),
            pltpu.SemaphoreType.DMA((8, 4)),
            pltpu.SemaphoreType.DMA((8, 4)),
            pltpu.SemaphoreType.DMA((4,)),
        ],
        compiler_params=pltpu.CompilerParams(
            collective_id=0, has_side_effects=True, vmem_limit_bytes=52400 << 10
        ),
    )(p0, p1, m4, m5, material, speed_sq, admittance, bound_cell, bound_patch)
    return pl.pallas_call(
        hand_over,
        out_shape=shapes,
        in_specs=[vmem] * 3,
        out_specs=(anywhere,) * 3,
        scratch_shapes=[pltpu.SemaphoreType.DMA((3,))],
        compiler_params=pltpu.CompilerParams(vmem_limit_bytes=4 << 20),
    )(*results)


def solution(mesh):
    field = P("row", "col", None)
    return jax.shard_map(
        local,
        mesh=mesh,
        in_specs=(field,) * 5 + (P(), P("col", "row"), P("row", "col"), P("row", "col")),
        out_specs=(field, field, P("col", "row")),
        check_vma=False,
    )
```

```python
import jax
import jax.numpy as jnp
from jax import lax
from jax.experimental import pallas as pl
from jax.experimental.pallas import tpu as pltpu
from jax.sharding import PartitionSpec as P

MESH = pl.DeviceIdType.MESH
F32 = jnp.float32
BF16 = jnp.bfloat16
CX, CY, NZ = 16, 128, 128
SLOTS = 2048
ROWS = 32
COLS = 8
SHARE = 64
PX, PY = CX + 2, CY + 16
GROUP = 7
EDGE = 14
PAIR = 7
RIM = 512


def natural(step):
    return pl.ds(step, 8, 16)


def along(field, x, count, beside):
    value = field[pl.ds(x, count), 8 : 8 + CY, :].reshape(count * CY, NZ)
    high = value.astype(BF16)
    low = (value - high.astype(F32)).astype(BF16)
    return jnp.dot(
        jnp.concatenate([high, low], axis=1), beside[...], preferred_element_type=F32
    )


def around(field, x, tiles, sums):
    at = lambda plane, t: field[plane, pl.ds(8 + 8 * t, 8), :]
    line = {t: at(x, t) for t in range(tiles[0] - 1, tiles[-1] + 2)}
    found = []
    for t in tiles:
        here = line[t]
        total = (at(x - 1, t) + at(x + 1, t)) + (line[t - 1] + line[t + 1])
        found.append((t, here, total + sums(t) - 6.0 * here))
    return found


def put(field, x, t, value):
    field[x, pl.ds(8 + 8 * t, 8), :] = value
    if t == 15:
        field[x, 1:8, :] = value[0:7]
    if t == 0:
        field[x, CY + 8 : CY + 15, :] = value[1:8]


def kernel(
    p0_in, p1_in, m4_in, m5_in, mat_in, speed, adm, cell, patch,
    g0_out, g1_out, pg_out,
    kinds, raw_p1, raw_p0, raw_m5, raw_m4,
    f0, f1, f2, f3, f4, f5, f6, f7,
    c2, q, before, base0, base1, diff0, diff1, w0, w1, w2, w3, last,
    zs, zs_last, beside, side, rt, bt, vt, gt, rt_rim, gt_rim, own, table, parts, arrived,
    load_sem, send_sem, recv_sem, share_sem,
):
    fields = (f0, f1, f2, f3, f4, f5, f6, f7)
    bases = (base0, base1)
    diffs = (diff0, diff1)
    weights = (w0, w1, w2, w3)
    row = lax.axis_index("row")
    col = lax.axis_index("col")

    pairs = (
        (p1_in, raw_p1), (mat_in, kinds), (p0_in, raw_p0), (m5_in, raw_m5), (m4_in, raw_m4)
    )
    loads = [
        pltpu.make_async_copy(ref, raw, load_sem.at[n]) for n, (ref, raw) in enumerate(pairs)
    ]
    for load in loads:
        load.start()

    barrier = pltpu.get_barrier_semaphore()

    def greet(step, carry):
        pl.semaphore_signal(
            barrier, inc=1, device_id=(lax.rem(row + step, ROWS), col), device_id_type=MESH
        )
        return carry

    lax.fori_loop(1, ROWS, greet, 0)
    for step in (1, COLS - 1):
        pl.semaphore_signal(
            barrier, inc=1, device_id=(row, lax.rem(col + step, COLS)), device_id_type=MESH
        )

    zero_plane = jnp.zeros((CY, NZ), F32)
    zero_row = jnp.zeros((CX, 1, NZ), F32)

    @pl.when(row == 0)
    def _():
        for f in range(8):
            fields[f][0, 8 : 8 + CY, :] = zero_plane

    @pl.when(row == ROWS - 1)
    def _():
        for f in range(8):
            fields[f][PX - 1, 8 : 8 + CY, :] = zero_plane

    @pl.when(col == 0)
    def _():
        for f in range(8):
            fields[f][1 : 1 + CX, 0:1, :] = zero_row

    @pl.when(col == COLS - 1)
    def _():
        for f in range(8):
            fields[f][1 : 1 + CX, PY - 1 : PY, :] = zero_row

    own[...] = jnp.zeros_like(own)
    own[0, :, 0:SHARE] = adm[...]
    table[pl.ds(row, 1)] = own[...]

    pl.semaphore_wait(barrier, ROWS + 1)

    sides = (
        (row < ROWS - 1, (row + 1, col)),
        (row > 0, (row - 1, col)),
        (col < COLS - 1, (row, col + 1)),
        (col > 0, (row, col - 1)),
    )
    comes = (row > 0, row < ROWS - 1, col > 0, col < COLS - 1)

    def copies(f):
        field = fields[f]
        pairs = (
            (field.at[CX, 8 : 8 + CY, :], field.at[0, 8 : 8 + CY, :]),
            (field.at[1, 8 : 8 + CY, :], field.at[PX - 1, 8 : 8 + CY, :]),
            (field.at[1 : 1 + CX, CY + 7 : CY + 8, :], field.at[1 : 1 + CX, 0:1, :]),
            (field.at[1 : 1 + CX, 8:9, :], field.at[1 : 1 + CX, PY - 1 : PY, :]),
        )
        if f == 0:
            pairs = (
                (p1_in.at[CX - 1], side.at[0]),
                (p1_in.at[0], side.at[1]),
                (p1_in.at[:, CY - 1 : CY, :], pairs[2][1]),
                (p1_in.at[:, 0:1, :], pairs[3][1]),
            )
        return [
            pltpu.make_async_remote_copy(
                src, dst, send_sem.at[f, d], recv_sem.at[f, d],
                device_id=sides[d][1], device_id_type=MESH,
            )
            for d, (src, dst) in enumerate(pairs)
        ]

    def send(f):
        for d, copy in enumerate(copies(f)):
            pl.when(sides[d][0])(copy.start)

    def receive(f):
        for d, copy in enumerate(copies(f)):
            pl.when(comes[d])(copy.wait_recv)

    def sent(f):
        for d, copy in enumerate(copies(f)):
            pl.when(sides[d][0])(copy.wait_send)

    send(0)

    def share(source, sem):
        def start(step, carry):
            to = lax.rem(row + step, ROWS)
            pltpu.make_async_remote_copy(
                source(to), (table if sem == 0 else arrived).at[pl.ds(row, 1)],
                share_sem.at[2 * sem], share_sem.at[2 * sem + 1],
                device_id=(to, col), device_id_type=MESH,
            ).start()
            return carry

        lax.fori_loop(1, ROWS, start, 0)

    def shared(buffer, which):
        rest = buffer.at[pl.ds(0, ROWS - 1)]
        pltpu.make_async_copy(rest, rest, share_sem.at[which]).wait()

    share(lambda to: own, 0)

    cells = cell[...]
    spots = patch[...]
    depth = cells & (NZ - 1)
    y = (cells >> 7) & (CY - 1)
    line = (cells >> 14) * CY + (y & 15) * 8 + (y >> 4)
    owner = spots >> 6
    place = spots & (SHARE - 1)

    def build(block, carry):
        start = pl.multiple_of(block * 16, 16)
        index = lax.broadcasted_iota(jnp.int32, (16, SLOTS), 0) + start
        rt[pl.ds(start, 16), :] = jnp.where(index == line, 1.0, 0.0).astype(BF16)
        return carry

    lax.fori_loop(0, SLOTS // 16, build, 0)
    plane = cells >> 14
    inner = jnp.where((y & 15) == 0, 256, 384) + 8 * (plane - 1) + (y >> 4)
    inner = jnp.where(((y & 15) == 0) | ((y & 15) == 15), inner, -1)
    ends_line = jnp.where(plane == 0, line, line - (CX - 2) * CY)
    rim = jnp.where((plane == 0) | (plane == CX - 1), ends_line, inner)
    rim = jnp.where(cells < 0, -1, rim)

    def build_rim(block, carry):
        start = pl.multiple_of(block * 16, 16)
        index = lax.broadcasted_iota(jnp.int32, (16, SLOTS), 0) + start
        rt_rim[pl.ds(start, 16), :] = jnp.where(index == rim, 1.0, 0.0).astype(BF16)
        return carry

    lax.fori_loop(0, RIM // 16, build_rim, 0)
    index = lax.broadcasted_iota(jnp.int32, (2 * NZ, NZ), 0) & (NZ - 1)
    apart = index - lax.broadcasted_iota(jnp.int32, (2 * NZ, NZ), 1)
    beside[...] = jnp.where((apart == 1) | (apart == -1), 1.0, 0.0).astype(BF16)
    index = lax.broadcasted_iota(jnp.int32, (NZ, SLOTS), 0)
    bt[...] = jnp.where(index == place, 1.0, 0.0).astype(BF16)

    loads[0].wait()
    loads[1].wait()
    speeds = [speed[n] for n in range(8)]

    def arrange(x, carry):
        values = [raw_p1[x, natural(t), :] for t in range(16)]
        sorts = [kinds[x, natural(t), :] for t in range(16)]
        for t in range(16):
            put(f0, x + 1, t, values[t])
        for t in range(16):
            value = jnp.full((8, NZ), speeds[0], F32)
            for n in range(1, 8):
                value = jnp.where(sorts[t] == n, speeds[n], value)
            c2[x, pl.ds(8 * t, 8), :] = value
        return carry

    lax.fori_loop(0, CX, arrange, 0)

    loads[2].wait()
    loads[3].wait()
    loads[4].wait()

    def arrange_rest(x, carry):
        values = [raw_p0[x, natural(t), :] for t in range(16)]
        for t in range(16):
            before[x, pl.ds(8 * t, 8), :] = values[t]
        return carry

    lax.fori_loop(0, CX, arrange_rest, 0)

    shared(table, 1)
    shared(table, 0)
    strip = 0.25 * table[:, 0, :]
    strip_high = strip.astype(BF16)
    strip_low = (strip - strip_high.astype(F32)).astype(BF16)
    found = jnp.dot(
        jnp.concatenate([strip_high, strip_low], axis=0), bt[...], preferred_element_type=F32
    )
    found = found[:ROWS] + found[ROWS:]
    index = lax.broadcasted_iota(jnp.int32, (ROWS, SLOTS), 0)
    slot = jnp.sum(jnp.where(index == owner, found, 0.0), axis=0, keepdims=True)
    slot_high = slot.astype(BF16).astype(F32)
    slot_low = slot - slot_high
    index = lax.broadcasted_iota(jnp.int32, (NZ, SLOTS), 0)
    vt[0:NZ, :] = jnp.where(index == depth, slot_high, 0.0).astype(BF16)
    vt[NZ : 2 * NZ, :] = jnp.where(index == depth, slot_low, 0.0).astype(BF16)

    def spread(pair, carry):
        start = pl.multiple_of(pair * 256, 256)
        both = lax.dot_general(
            rt[pl.ds(start, 256), :], vt[...], (((1,), (1,)), ((), ())), preferred_element_type=F32
        )
        for half in range(2):
            x = 2 * pair + half
            for t in range(16):
                at = half * CY + 8 * t
                gamma = both[at : at + 8, 0:NZ] + both[at : at + 8, NZ : 2 * NZ]
                here = pl.ds(8 * t, 8)
                scale = 1.0 / (1.0 + gamma)
                high = raw_m5[x, natural(t), :]
                low = raw_m4[x, natural(t), :]
                weight = scale * high
                twice = 2.0 * weight
                q[x, here, :] = scale
                w0[x, here, :] = weight
                put(f4, x + 1, t, c2[x, here, :] * weight)
                base0[x, here, :] = low + twice
                diff0[x, here, :] = high - twice
        return carry

    lax.fori_loop(0, CX // 2, spread, 0, unroll=4)
    send(4)

    def forward(k):
        def group(work):
            found = []
            for x, tiles, sums in work:
                for t, here, change in around(fields[k - 1], x, tiles, sums):
                    at = pl.ds(8 * t, 8)
                    if k == 1:
                        old = before[x - 1, at, :]
                    else:
                        old = fields[k - 2][x, pl.ds(8 + 8 * t, 8), :]
                    new = old + q[x - 1, at, :] * (2.0 * (here - old) + c2[x - 1, at, :] * change)
                    found.append((x, t, new))
            for x, t, new in found:
                if k == 4:
                    last[x - 1, pl.ds(8 * t, 8), :] = new
                else:
                    put(fields[k], x, t, new)

        return fields[k - 1], group, (zs_last if k == 4 else zs)

    def adjoint(k):
        f = 8 - k
        base, next_base = bases[k % 2], bases[1 - k % 2]
        diff, next_diff = diffs[k % 2], diffs[1 - k % 2]

        def group(work):
            found = []
            for x, tiles, sums in work:
                for t, here, change in around(fields[f], x, tiles, sums):
                    at = pl.ds(8 * t, 8)
                    high = base[x - 1, at, :] + change
                    if k == 1:
                        found.append((x, t, high))
                        continue
                    weight = q[x - 1, at, :] * high
                    twice = 2.0 * weight
                    found.append(
                        (x, t, weight, c2[x - 1, at, :] * weight,
                         diff[x - 1, at, :] + twice, high - twice)
                    )
            for x, t, *values in found:
                at = pl.ds(8 * t, 8)
                if k == 1:
                    g1_out[x - 1, natural(t), :] = values[0]
                    continue
                weights[f - 3][x - 1, at, :] = values[0]
                put(fields[f + 1], x, t, values[1])
                next_base[x - 1, at, :] = values[2]
                if k == 2:
                    g0_out[x - 1, natural(t), :] = values[3]
                else:
                    next_diff[x - 1, at, :] = values[3]

        return fields[f], group, zs

    def inside(step):
        field, group, kept = step

        def body(n, carry):
            x = 2 + PAIR * n
            sums = along(field, x, PAIR, beside)
            for i in range(PAIR):
                tile = lambda t, i=i: sums[CY * i + 8 * t : CY * i + 8 * t + 8]
                for t in (0, 15):
                    kept[x + i - 1, pl.ds(8 * t, 8), :] = tile(t)
                for start in range(1, 15, GROUP):
                    group([(x + i, range(start, start + GROUP), tile)])
            return carry

        for x in (1, CX):
            kept[x - 1] = along(field, x, 1, beside)
        lax.fori_loop(0, 14 // PAIR, body, 0)

    def outside(step):
        field, group, kept = step

        def tile(x):
            return lambda t: kept[x - 1, pl.ds(8 * t, 8), :]

        def ends(n, carry):
            x = 1 + n * (CX - 1)
            for start in range(0, 16, 8):
                group([(x, range(start, start + 8), tile(x))])
            return carry

        def edges(n, carry):
            x = 2 + EDGE * n
            for t in (0, 15):
                group([(x + i, (t,), tile(x + i)) for i in range(EDGE)])
            return carry

        lax.fori_loop(0, 2, ends, 0)
        lax.fori_loop(0, 14 // EDGE, edges, 0)

    inside(forward(1))
    receive(0)
    for n, plane, there in ((0, 0, comes[0]), (1, PX - 1, comes[1])):
        def place_side(n=n, plane=plane):
            for t in range(16):
                f0[plane, pl.ds(8 + 8 * t, 8), :] = side[n, natural(t), :]

        pl.when(there)(place_side)
    outside(forward(1))
    send(1)

    for k in (2, 3):
        level = 6 - k
        step = adjoint(level)
        inside(step)
        receive(8 - level)
        outside(step)
        send(9 - level)
        step = forward(k)
        inside(step)
        receive(k - 1)
        outside(step)
        send(k)

    def product(x, t):
        at = pl.ds(8 * t, 8)
        inner = pl.ds(8 + 8 * t, 8)
        states = [before[x, at, :]]
        states += [fields[k][x + 1, inner, :] for k in range(4)]
        states.append(last[x, at, :])
        total = w3[x, at, :] * (states[0] - states[2])
        for k in (2, 3, 4):
            total = total + weights[4 - k][x, at, :] * (states[k - 1] - states[k + 1])
        return 0.25 * total

    def turn(target, lane, tiles):
        turned = jnp.concatenate(tiles, axis=0).T
        high = turned.astype(BF16)
        target[0:NZ, lane] = high
        target[NZ : 2 * NZ, lane] = (turned - high.astype(F32)).astype(BF16)

    def collect(x, carry):
        none = jnp.zeros((8, NZ), F32)
        tiles = [none] + [product(x, t) for t in range(1, 15)] + [none]
        turn(gt, pl.ds(pl.multiple_of(x * CY, CY), CY), tiles)
        return carry

    def pick(source, start, stop, table_of_rows, lanes):
        picked = jnp.dot(
            source[:, start:stop], table_of_rows[start:stop, lanes], preferred_element_type=F32
        )
        picked = picked[:NZ] + picked[NZ:]
        index = lax.broadcasted_iota(jnp.int32, (NZ, 256), 0)
        return jnp.sum(
            jnp.where(index == depth[:, lanes], picked, 0.0), axis=0, keepdims=True
        )

    step = adjoint(2)
    ahead = forward(4)
    inside(step)
    inside(ahead)
    lax.fori_loop(1, CX - 1, collect, 0, unroll=2)
    early = [
        pick(gt, CY, (CX - 1) * CY, rt, slice(256 * c, 256 * c + 256))
        for c in range(SLOTS // 256)
    ]
    receive(6)
    outside(step)
    send(7)
    receive(3)
    outside(ahead)
    none = jnp.zeros((8, NZ), F32)
    turn(gt_rim, slice(0, CY), [product(0, t) for t in range(16)])
    turn(gt_rim, slice(CY, 2 * CY), [product(CX - 1, t) for t in range(16)])
    for n, t in ((2, 0), (3, 15)):
        tiles = [product(x, t) for x in range(1, CX - 1)] + [none, none]
        turn(gt_rim, slice(n * CY, (n + 1) * CY), tiles)
    total = jnp.zeros((2 * ROWS, NZ), F32)
    for chunk in range(SLOTS // 256):
        lanes = slice(256 * chunk, 256 * chunk + 256)
        value = early[chunk] + pick(gt_rim, 0, RIM, rt_rim, lanes)
        high = value.astype(BF16).astype(F32)
        low = value - high
        index = lax.broadcasted_iota(jnp.int32, (ROWS, 256), 0)
        mine = index == owner[:, lanes]
        both = jnp.concatenate(
            [jnp.where(mine, high, 0.0), jnp.where(mine, low, 0.0)], axis=0
        ).astype(BF16)
        total = total + lax.dot_general(
            both, bt[:, lanes], (((1,), (1,)), ((), ())), preferred_element_type=F32
        )
    parts[:, 0, :] = total[:ROWS] + total[ROWS:]
    arrived[pl.ds(row, 1)] = parts[pl.ds(row, 1)]
    share(lambda to: parts.at[pl.ds(to, 1)], 1)

    step = adjoint(1)
    inside(step)
    receive(7)
    outside(step)

    shared(arrived, 3)
    shared(arrived, 2)
    pg_out[...] = jnp.sum(arrived[...], axis=0)[:, 0:SHARE]
    for f in range(8):
        sent(f)


def hand_over(g0_in, g1_in, pg_in, g0_out, g1_out, pg_out, sem):
    pairs = ((g0_in, g0_out), (g1_in, g1_out), (pg_in, pg_out))
    copies = [pltpu.make_async_copy(src, dst, sem.at[n]) for n, (src, dst) in enumerate(pairs)]
    for copy in copies:
        copy.start()
    for copy in copies:
        copy.wait()


def local(p0, p1, m4, m5, material, speed_sq, admittance, bound_cell, bound_patch):
    block = (CX, CY, NZ)
    anywhere = pl.BlockSpec(memory_space=pl.ANY)
    far = pl.BlockSpec(memory_space=pltpu.HBM)
    vmem = pl.BlockSpec(memory_space=pltpu.VMEM)
    shapes = (
        jax.ShapeDtypeStruct(block, F32),
        jax.ShapeDtypeStruct(block, F32),
        jax.ShapeDtypeStruct((1, SHARE), F32),
    )
    results = pl.pallas_call(
        kernel,
        out_shape=shapes,
        in_specs=[far] * 5 + [pl.BlockSpec(memory_space=pltpu.SMEM)] + [vmem] * 3,
        out_specs=(vmem,) * 3,
        scratch_shapes=[pltpu.VMEM(block, jnp.int32)]
        + [pltpu.VMEM(block, F32)] * 4
        + [pltpu.VMEM((PX, PY, NZ), F32)] * 8
        + [pltpu.VMEM(block, F32)] * 12
        + [
            pltpu.VMEM(block, F32),
            pltpu.VMEM(block, F32),
            pltpu.VMEM((2 * NZ, NZ), BF16),
            pltpu.VMEM((2, CY, NZ), F32),
            pltpu.VMEM((SLOTS, SLOTS), BF16),
            pltpu.VMEM((NZ, SLOTS), BF16),
            pltpu.VMEM((2 * NZ, SLOTS), BF16),
            pltpu.VMEM((2 * NZ, SLOTS), BF16),
            pltpu.VMEM((RIM, SLOTS), BF16),
            pltpu.VMEM((2 * NZ, RIM), BF16),
            pltpu.VMEM((1, 1, NZ), F32),
            pltpu.VMEM((ROWS, 1, NZ), F32),
            pltpu.VMEM((ROWS, 1, NZ), F32),
            pltpu.VMEM((ROWS, 1, NZ), F32),
            pltpu.SemaphoreType.DMA((5,)),
            pltpu.SemaphoreType.DMA((8, 4)),
            pltpu.SemaphoreType.DMA((8, 4)),
            pltpu.SemaphoreType.DMA((4,)),
        ],
        compiler_params=pltpu.CompilerParams(
            collective_id=0, has_side_effects=True, vmem_limit_bytes=52400 << 10
        ),
    )(p0, p1, m4, m5, material, speed_sq, admittance, bound_cell, bound_patch)
    return pl.pallas_call(
        hand_over,
        out_shape=shapes,
        in_specs=[vmem] * 3,
        out_specs=(anywhere,) * 3,
        scratch_shapes=[pltpu.SemaphoreType.DMA((3,))],
        compiler_params=pltpu.CompilerParams(vmem_limit_bytes=4 << 20),
    )(*results)


def solution(mesh):
    field = P("row", "col", None)
    return jax.shard_map(
        local,
        mesh=mesh,
        in_specs=(field,) * 5 + (P(), P("col", "row"), P("row", "col"), P("row", "col")),
        out_specs=(field, field, P("col", "row")),
        check_vma=False,
    )
```
